32 devices in a mesh: dp: 4 (over y, x), section: 4 (over z), tensor: 2 (over core).
Axes of the slice: x: 2, y: 2, z: 4, core: 2. Of those that a mesh axis runs over, the one named last changes fastest.
Arguments:
- hidden: bfloat16 [32, 448, 768], P(('dp', 'section')), may hold values from -12 to 12
- enc_states: bfloat16 [32, 1536, 768], P('dp', 'section'), may hold values from -6 to 6
- out_grad: bfloat16 [32, 448, 768], P(('dp', 'section')), may hold values from -6 to 6
- text_len: int32 [32], P(('dp', 'section')), may hold values from 224 to 448, as said below
- audio_len: int32 [32], P(('dp', 'section')), may hold values from 384 to 1536, as said below
- group_id: int32 [32], P(('dp', 'section')), may hold values from 0 to 7
- group_weight: float32 [8], replicated, may hold values from 0.5 to 2
- norm_gain: bfloat16 [1, 3, 768], replicated, may hold values from 0.5 to 1.5
- norm_bias: bfloat16 [1, 3, 768], replicated, may hold values from -1.75 to 1.75
- attention_in: bfloat16 [1, 2, 3, 768, 768], P(None, None, None, None, 'tensor'), may hold values from -0.21875 to 0.21875
- query_value_bias: bfloat16 [1, 2, 2, 768], P(None, None, None, 'tensor'), may hold values from -1.75 to 1.75
- attention_out: bfloat16 [1, 2, 768, 768], P(None, None, 'tensor'), may hold values from -1.25 to 1.25
- attention_out_bias: bfloat16 [1, 2, 768], replicated, may hold values from -1.75 to 1.75
- mlp_in: bfloat16 [1, 768, 3072], P(None, None, 'tensor'), may hold values from -0.21875 to 0.21875
- mlp_in_bias: bfloat16 [1, 3072], P(None, 'tensor'), may hold values from -1.75 to 1.75
- mlp_out: bfloat16 [1, 3072, 768], P(None, 'tensor'), may hold values from -0.109375 to 0.109375
- mlp_out_bias: bfloat16 [1, 768], replicated, may hold values from -1.75 to 1.75
- final_gain: bfloat16 [768], replicated, may hold values from 0.5 to 1.5
- final_bias: bfloat16 [768], replicated, may hold values from -1.75 to 1.75
Outputs:
- decoded: bfloat16 [32, 448, 768], P(('dp', 'section'))
- input_grad: bfloat16 [32, 448, 768], P(('dp', 'section'))
- residual_rms: float32 [2], replicated
- grad_norm_gain: float32 [1, 3, 768], replicated
- grad_norm_bias: float32 [1, 3, 768], replicated
- grad_attention_in: float32 [1, 2, 3, 768, 768], P(None, None, None, ('dp', 'section'), 'tensor')
- grad_query_value_bias: float32 [1, 2, 2, 768], P(None, None, None, 'tensor')
- grad_attention_out: float32 [1, 2, 768, 768], P(None, None, 'tensor', ('dp', 'section'))
- grad_attention_out_bias: float32 [1, 2, 768], replicated
- grad_mlp_in: float32 [1, 768, 3072], P(None, ('dp', 'section'), 'tensor')
- grad_mlp_in_bias: float32 [1, 3072], P(None, 'tensor')
- grad_mlp_out: float32 [1, 3072, 768], P(None, 'tensor', ('dp', 'section'))
- grad_mlp_out_bias: float32 [1, 768], replicated
- grad_final_gain: float32 [768], replicated
- grad_final_bias: float32 [768], replicated
The draws below stay inside these ranges and needn't reach their ends.
Inputs may be any that keep to these rules, and one draw needn't show every extreme that they name: `text_len`: each transcript's valid tokens are its first positions; some transcript has all 448. `audio_len`: each recording's valid frames are its first slots; some recording fills all 1536.
All inputs are finite; a program needn't handle non-finite values.
Results may differ from the reference program's by a relative error of at most 0.023.
Values may be sent and summed in bfloat16 or wider, within the bound.
No kernel may reach another device: no remote copies, remote signals or barrier semaphores. Data moves between devices by JAX's collectives and lax.ppermute only.
A program may use at most 320 MiB of HBM per device.

```python
import math
import jax
import jax.numpy as jnp
from jax import lax

D = 768
HEAD = 64
FF = 3072
LAYERS = 1
LEN = 448
FRAMES = 1536
GROUPS = 8
SEQS = 32


def draw_hidden(key, part):
    key = jax.random.fold_in(key, 11)
    scale_key, value_key = jax.random.split(key)
    factors = jnp.exp(jax.random.uniform(scale_key, (SEQS, 1, 1), jnp.float32, -1.1, 1.1))
    base_values = jnp.clip(jax.random.normal(value_key, (SEQS, LEN, D), jnp.float32), -4.0, 4.0)
    return (factors * base_values).astype(jnp.bfloat16)


def draw_text_len(key, part):
    key = jax.random.fold_in(key, 23)
    pick_key, count_key = jax.random.split(key)
    counts = jax.random.randint(count_key, (SEQS,), LEN // 2, LEN + 1)
    longest = jax.random.randint(pick_key, (), 0, SEQS)
    return jnp.where(jnp.arange(SEQS) == longest, LEN, counts).astype(jnp.int32)


def draw_audio_len(key, part):
    key = jax.random.fold_in(key, 37)
    pick_key, count_key = jax.random.split(key)
    counts = jax.random.randint(count_key, (SEQS,), FRAMES // 4, FRAMES + 1)
    longest = jax.random.randint(pick_key, (), 0, SEQS)
    return jnp.where(jnp.arange(SEQS) == longest, FRAMES, counts).astype(jnp.int32)


def place_ends(values, stream_key, least, largest):
    longest = values.shape.index(max(values.shape))
    spots = []
    for shift in (0, 1):
        where = [jax.random.randint(jax.random.fold_in(stream_key, axis), (), 0, length) for axis, length in enumerate(values.shape)]
        where[longest] = (where[longest] + shift) % values.shape[longest]
        spots.append(tuple(where))
    return values.at[spots[0]].set(least).at[spots[1]].set(largest)


def level_of(stream_key, extent, shards, low, high):
    level = 1.0
    for position, blocks in shards:
        steps = jax.random.uniform(jax.random.fold_in(jax.random.fold_in(stream_key, 6), position), (blocks,), jnp.float32, low / len(shards), high / len(shards))
        level = level * jnp.repeat(jnp.exp(steps), extent[position] // blocks).reshape((-1,) + (1,) * (len(extent) - 1 - position))
    return level


def scatter_about(own_key, extent, scale, reach, shards=(), held_as=jnp.bfloat16):
    array = scale * jax.random.normal(own_key, extent, jnp.float32)
    if shards:
        array = array * level_of(own_key, extent, shards, -0.22, 0.18)
    return jnp.clip(array, -reach, reach).astype(held_as)


def setup_inputs(seed: int = 0) -> dict:
    keys = jax.random.split(jax.random.key(seed), 20)
    hidden = draw_hidden(jax.random.fold_in(keys[19], 71), 0)
    enc_states = scatter_about(keys[1], (SEQS, FRAMES, D), 1.0, 6.0, ((0, 4), (1, 4)))
    out_grad = scatter_about(keys[2], (SEQS, LEN, D), 1.0, 6.0, ((0, 16),))
    text_len = draw_text_len(jax.random.fold_in(keys[19], 71), 0)
    audio_len = draw_audio_len(jax.random.fold_in(keys[19], 71), 0)
    group_id = place_ends(jax.random.randint(keys[5], (SEQS,), 0, GROUPS), jax.random.fold_in(keys[5], 1), 0, GROUPS - 1).astype(jnp.int32)
    group_weight = jnp.clip(jnp.exp(jax.random.uniform(keys[6], (GROUPS,), jnp.float32, math.log(0.5), math.log(2.0))), 0.5, 2.0)
    norm_gain = jnp.clip(1.0 + 0.1 * jax.random.normal(keys[7], (LAYERS, 3, D), jnp.float32), 0.5, 1.5).astype(jnp.bfloat16)
    norm_bias = scatter_about(keys[8], (LAYERS, 3, D), 0.3, 1.75)
    attention_in = scatter_about(keys[9], (LAYERS, 2, 3, D, D), D ** -0.5, 0.21875, ((4, 2),))
    query_value_bias = scatter_about(keys[10], (LAYERS, 2, 2, D), 0.3, 1.75, ((3, 2),))
    attention_out = scatter_about(keys[11], (LAYERS, 2, D, D), (D // 32) ** -0.5, 1.25, ((2, 2),))
    attention_out_bias = scatter_about(keys[12], (LAYERS, 2, D), 0.3, 1.75)
    mlp_in = scatter_about(keys[13], (LAYERS, D, FF), D ** -0.5, 0.21875, ((2, 2),))
    mlp_in_bias = scatter_about(keys[14], (LAYERS, FF), 0.3, 1.75, ((1, 2),))
    mlp_out = scatter_about(keys[15], (LAYERS, FF, D), FF ** -0.5, 0.109375, ((1, 2),))
    mlp_out_bias = scatter_about(keys[16], (LAYERS, D), 0.3, 1.75)
    final_gain = jnp.clip(1.0 + 0.1 * jax.random.normal(keys[17], (D,), jnp.float32), 0.5, 1.5).astype(jnp.bfloat16)
    final_bias = scatter_about(keys[18], (D,), 0.3, 1.75)
    return dict(hidden=hidden, enc_states=enc_states, out_grad=out_grad, text_len=text_len, audio_len=audio_len, group_id=group_id, group_weight=group_weight, norm_gain=norm_gain, norm_bias=norm_bias, attention_in=attention_in, query_value_bias=query_value_bias, attention_out=attention_out, attention_out_bias=attention_out_bias, mlp_in=mlp_in, mlp_in_bias=mlp_in_bias, mlp_out=mlp_out, mlp_out_bias=mlp_out_bias, final_gain=final_gain, final_bias=final_bias)


EPS = 1e-05
NEGATIVE = -1e+30
HIGH = lax.Precision.HIGHEST

@jax.custom_vjp
def low(v):
    return lax.optimization_barrier(v.astype(jnp.bfloat16)).astype(jnp.float32)

@jax.custom_vjp
def low_back(v):
    return v

def low_keep(v):
    return (low(v), None)

def low_pass(kept, grad):
    return (grad,)

def back_keep(v):
    return (v, None)

def back_low(kept, grad):
    return (low(grad),)
low.defvjp(low_keep, low_pass)
low_back.defvjp(back_keep, back_low)

def lowered(values):
    return low_back(low(values))

def matmul(former, latter):
    return jnp.dot(former, latter, precision=HIGH)

def norm_forward(row_block, norm_scale, norm_shift):
    centred = row_block - lax.optimization_barrier(jnp.mean(row_block, -1, keepdims=True))
    spread = lax.optimization_barrier(jnp.mean(centred * centred, -1, keepdims=True))
    return centred * lax.rsqrt(spread + EPS) * norm_scale + norm_shift

def split_heads(values):
    return values.reshape(values.shape[0], values.shape[1] // HEAD, HEAD)

def attend(queries, key_rows, value_rows, allowed):
    scores = jnp.einsum('thd,fhd->htf', split_heads(queries), split_heads(key_rows), precision=HIGH)
    scores = low_back(scores)
    scores = jnp.where(allowed[None], scores, NEGATIVE)
    weights = low(jax.nn.softmax(scores, axis=-1))
    mixture = jnp.einsum('htf,fhd->thd', weights, split_heads(value_rows), precision=HIGH)
    return lowered(mixture.reshape(queries.shape))

def decoder_sequence(params, seq_rows, frames, audio_count, text_count):
    norm_gain, norm_bias, attention_in, query_value_bias, attention_out, attention_out_bias, mlp_in, mlp_in_bias, mlp_out, mlp_out_bias, final_gain, final_bias = params
    head_scale = HEAD ** (-0.5)
    positions = jnp.arange(LEN)
    causal = positions[:, None] >= positions[None, :]
    heard_mask = (jnp.arange(FRAMES) < audio_count)[None, :]
    valid_rows = (positions < text_count).astype(jnp.float32)
    residual = seq_rows
    squares = [jnp.sum(valid_rows[:, None] * residual * residual)]
    for layer_id in range(LAYERS):
        normed = low(norm_forward(residual, norm_gain[layer_id, 0], norm_bias[layer_id, 0]))
        queries = lowered((matmul(normed, attention_in[layer_id, 0, 0]) + query_value_bias[layer_id, 0, 0]) * head_scale)
        key_rows = lowered(matmul(normed, attention_in[layer_id, 0, 1]))
        value_rows = lowered(matmul(normed, attention_in[layer_id, 0, 2]) + query_value_bias[layer_id, 0, 1])
        mixture = attend(queries, key_rows, value_rows, causal)
        residual = residual + low_back(matmul(mixture, attention_out[layer_id, 0]) + attention_out_bias[layer_id, 0])
        normed = low(norm_forward(residual, norm_gain[layer_id, 1], norm_bias[layer_id, 1]))
        queries = lowered((matmul(normed, attention_in[layer_id, 1, 0]) + query_value_bias[layer_id, 1, 0]) * head_scale)
        key_rows = lowered(matmul(frames, attention_in[layer_id, 1, 1]))
        value_rows = lowered(matmul(frames, attention_in[layer_id, 1, 2]) + query_value_bias[layer_id, 1, 1])
        mixture = attend(queries, key_rows, value_rows, heard_mask)
        residual = residual + low_back(matmul(mixture, attention_out[layer_id, 1]) + attention_out_bias[layer_id, 1])
        normed = low(norm_forward(residual, norm_gain[layer_id, 2], norm_bias[layer_id, 2]))
        pre_act = low_back(matmul(normed, mlp_in[layer_id]) + mlp_in_bias[layer_id])
        activated = low(jax.nn.gelu(pre_act, approximate=False))
        residual = residual + low_back(matmul(activated, mlp_out[layer_id]) + mlp_out_bias[layer_id])
        squares.append(jnp.sum(valid_rows[:, None] * residual * residual))
    return (norm_forward(residual, final_gain, final_bias), jnp.stack(squares))

def reference(hidden, enc_states, out_grad, text_len, audio_len, group_id, group_weight, norm_gain, norm_bias, attention_in, query_value_bias, attention_out, attention_out_bias, mlp_in, mlp_in_bias, mlp_out, mlp_out_bias, final_gain, final_bias):
    params = tuple((stored.astype(jnp.float32) for stored in (norm_gain, norm_bias, attention_in, query_value_bias, attention_out, attention_out_bias, mlp_in, mlp_in_bias, mlp_out, mlp_out_bias, final_gain, final_bias)))
    hidden_full = hidden.astype(jnp.float32)

    def forward_all(rows_all, params_all):

        def one_sequence(seq_items):
            seq_rows, frames, audio_count, text_count = seq_items
            return decoder_sequence(params_all, seq_rows, frames.astype(jnp.float32), audio_count, text_count)
        return lax.map(jax.checkpoint(one_sequence), (rows_all, enc_states, audio_len, text_len))
    (outputs, squares), pullback = jax.vjp(forward_all, hidden_full, params)
    positions = jnp.arange(LEN)
    valid_rows = (positions[None, :] < text_len[:, None]).astype(jnp.float32)
    row_weight = group_weight[group_id]
    cotangent = out_grad.astype(jnp.float32) * (row_weight[:, None] * valid_rows)[:, :, None]
    grad_hidden, grad_params = pullback((cotangent, jnp.zeros_like(squares)))
    token_count = jnp.sum(text_len).astype(jnp.float32)
    residual_rms = jnp.sqrt(lax.optimization_barrier(jnp.sum(squares, 0)) / (token_count * D))
    return (outputs.astype(jnp.bfloat16), grad_hidden.astype(jnp.bfloat16), residual_rms, grad_params[0], grad_params[1], grad_params[2], grad_params[3], grad_params[4], grad_params[5], grad_params[6], grad_params[7], grad_params[8], grad_params[9], grad_params[10], grad_params[11])
```

```python
import jax
import jax.numpy as jnp
from jax import lax
from jax.sharding import PartitionSpec as P

HEAD = 64
EPS = 1e-05
NEGATIVE = -1e30
BF = jnp.bfloat16
F32 = jnp.float32


def norm_parts(rows):
    centred = rows - jnp.mean(rows, -1, keepdims=True)
    rstd = lax.rsqrt(jnp.mean(centred * centred, -1, keepdims=True) + EPS)
    return centred * rstd, rstd


def norm_back(grad, normal, rstd, gain):
    scaled = grad * gain
    return (
        rstd
        * (
            scaled
            - jnp.mean(scaled, -1, keepdims=True)
            - normal * jnp.mean(scaled * normal, -1, keepdims=True)
        ),
        jnp.sum(grad * normal, 0),
        jnp.sum(grad, 0),
    )


def gelu_exact(values):
    return jax.nn.gelu(values, approximate=False)


def mm(a, b):
    return jnp.dot(a, b, preferred_element_type=F32)


def mm_tn(a, b):
    return lax.dot_general(a, b, (((0,), (0,)), ((), ())), preferred_element_type=F32)


def mm_nt(a, b):
    return lax.dot_general(a, b, (((1,), (1,)), ((), ())), preferred_element_type=F32)


def colsum(values):
    return jnp.sum(values, 0, dtype=F32)


def heads_of(values):
    return values.reshape(values.shape[0], values.shape[1] // HEAD, HEAD)


def score_block(queries, key_rows, allowed):
    scores = jnp.einsum(
        "thd,fhd->htf", heads_of(queries), heads_of(key_rows), preferred_element_type=F32
    )
    return jnp.where(allowed[None], scores, NEGATIVE)


def attend_forward(queries, key_rows, value_rows, allowed):
    scores = score_block(queries, key_rows, allowed)
    row_max = jnp.max(scores, -1, keepdims=True)
    powers = jnp.exp(scores - row_max)
    row_total = jnp.sum(powers, -1, keepdims=True)
    weights = (powers / row_total).astype(BF)
    mixture = jnp.einsum("htf,fhd->thd", weights, heads_of(value_rows), preferred_element_type=F32)
    return mixture.reshape(queries.shape).astype(BF), (row_max, row_total)


def attend_backward(queries, key_rows, value_rows, allowed, kept, grad_mixed):
    scores = score_block(queries, key_rows, allowed)
    row_max, row_total = kept
    weights = jnp.exp(scores - row_max) / row_total
    weights_low = weights.astype(BF)
    grad_heads = heads_of(grad_mixed)
    grad_weights = jnp.einsum(
        "thd,fhd->htf", grad_heads, heads_of(value_rows), preferred_element_type=F32
    )
    grad_values = jnp.einsum("htf,thd->fhd", weights_low, grad_heads, preferred_element_type=F32)
    grad_scores = weights * (grad_weights - jnp.sum(grad_weights * weights, -1, keepdims=True))
    scores_low = grad_scores.astype(BF)
    grad_queries = jnp.einsum(
        "htf,fhd->thd", scores_low, heads_of(key_rows), preferred_element_type=F32
    )
    grad_keys = jnp.einsum("htf,thd->fhd", scores_low, heads_of(queries), preferred_element_type=F32)
    return (
        grad_queries.reshape(queries.shape).astype(BF),
        grad_keys.reshape(key_rows.shape).astype(BF),
        grad_values.reshape(value_rows.shape).astype(BF),
    )


def swap(axis, bit):
    return [(i, i ^ (1 << bit)) for i in range(lax.axis_size(axis))]


def bits_of(axis):
    return (lax.axis_size(axis) - 1).bit_length()


def pick(values, axis, index):
    return lax.dynamic_index_in_dim(values, index, axis, keepdims=False)


def scatter_rows(values, flip):
    dims = [("dp", b) for b in reversed(range(bits_of("dp")))]
    dims += [("section", b) for b in reversed(range(bits_of("section")))]
    share = values.shape[0] // (1 << len(dims))
    cube = values.reshape((2,) * len(dims) + (share, values.shape[1]))
    dp_order = [d for d in dims if d[0] == "dp"]
    if not flip:
        dp_order = dp_order[::-1]
    for axis, bit in dp_order + [d for d in dims if d[0] == "section"][::-1]:
        where = dims.index((axis, bit))
        mine = (lax.axis_index(axis) >> bit) & 1
        sent = pick(cube, where, 1 - mine)
        kept = pick(cube, where, mine)
        got = lax.ppermute(sent, axis, swap(axis, bit))
        cube = (kept.astype(F32) + got.astype(F32)).astype(BF)
        dims.remove((axis, bit))
    return cube


def sum_all(values):
    for axis in ("dp", "section"):
        for bit in range(bits_of(axis)):
            values = values + lax.ppermute(values, axis, swap(axis, bit))
    return values


def per_device(
    hidden,
    enc_states,
    out_grad,
    text_len,
    audio_len,
    group_id,
    group_weight,
    norm_gain,
    norm_bias,
    attention_in,
    query_value_bias,
    attention_out,
    attention_out_bias,
    mlp_in,
    mlp_in_bias,
    mlp_out,
    mlp_out_bias,
    final_gain,
    final_bias,
):
    seq_length, width = hidden.shape[1:]
    sections = lax.axis_size("section")
    part = enc_states.shape[1]
    core = lax.axis_index("tensor")
    section = lax.axis_index("section")
    other = swap("tensor", 0)
    scale = HEAD ** (-0.5)

    frame_blocks = []
    slot_blocks = []
    for step in range(sections):
        target = lax.rem(section + step, sections)
        block = pick(enc_states, 0, 2 * target + core)
        if step:
            block = lax.ppermute(
                block, "section", [(i, (i + step) % sections) for i in range(sections)]
            )
        frame_blocks.append(block)
        source = lax.rem(section - step + sections, sections)
        slot_blocks.append(source * part + jnp.arange(part))

    def both(values, axis):
        return jnp.concatenate([values, lax.ppermute(values, "tensor", other)], axis)

    w_in = both(attention_in[0], 3)
    w_out = both(attention_out[0], 1)
    qv_bias = both(query_value_bias[0], 2).astype(F32)
    w_up = both(mlp_in[0], 1)
    up_bias = both(mlp_in_bias[0], 0).astype(F32)
    w_down = both(mlp_out[0], 0)
    gains = norm_gain[0].astype(F32)
    shifts = norm_bias[0].astype(F32)
    out_bias = attention_out_bias[0].astype(F32)
    down_bias = mlp_out_bias[0].astype(F32)
    last_gain = final_gain.astype(F32)
    last_shift = final_bias.astype(F32)

    text_count = pick(text_len, 0, core)
    audio_count = pick(audio_len, 0, core)
    group = pick(group_id, 0, core)
    positions = jnp.arange(seq_length)
    valid = (positions < text_count).astype(F32)[:, None]
    causal = positions[:, None] >= positions[None, :]
    x0 = pick(hidden, 0, core).astype(F32)
    square0 = jnp.sum(valid * x0 * x0)

    n0, r0 = norm_parts(x0)
    h0 = (n0 * gains[0] + shifts[0]).astype(BF)
    q0 = ((mm(h0, w_in[0, 0]) + qv_bias[0, 0]) * scale).astype(BF)
    k0 = mm(h0, w_in[0, 1]).astype(BF)
    v0 = (mm(h0, w_in[0, 2]) + qv_bias[0, 1]).astype(BF)
    o0, kept0 = attend_forward(q0, k0, v0, causal)
    x1 = x0 + (mm(o0, w_out[0]) + out_bias[0])

    n1, r1 = norm_parts(x1)
    h1 = (n1 * gains[1] + shifts[1]).astype(BF)
    q1 = ((mm(h1, w_in[1, 0]) + qv_bias[1, 0]) * scale).astype(BF)
    frames = jnp.concatenate(frame_blocks, 0)
    heard = (jnp.concatenate(slot_blocks, 0) < audio_count)[None, :]
    k1 = mm(frames, w_in[1, 1]).astype(BF)
    v1 = (mm(frames, w_in[1, 2]) + qv_bias[1, 1]).astype(BF)
    o1, kept1 = attend_forward(q1, k1, v1, heard)
    x2 = x1 + (mm(o1, w_out[1]) + out_bias[1])

    n2, r2 = norm_parts(x2)
    h2 = (n2 * gains[2] + shifts[2]).astype(BF)
    pre = mm(h2, w_up) + up_bias
    act, act_pull = jax.vjp(gelu_exact, pre)
    act = act.astype(BF)
    x3 = x2 + (mm(act, w_down) + down_bias)
    square1 = jnp.sum(valid * x3 * x3)

    n3, r3 = norm_parts(x3)
    decoded = (n3 * last_gain + last_shift).astype(BF)
    slots = jnp.arange(group_weight.shape[0])
    weight = jnp.sum(jnp.where(slots == group, group_weight, 0.0))
    cot = pick(out_grad, 0, core).astype(F32) * (weight * valid)
    g, d_last_gain, d_last_shift = norm_back(cot, n3, r3, last_gain)

    gb = g.astype(BF)
    d_down_bias = colsum(gb)
    d_down = mm_tn(gb, act)
    d_pre = act_pull(mm_nt(gb, w_down))[0].astype(BF)
    d_up_bias = colsum(d_pre)
    d_up = mm_tn(h2, d_pre)
    row, d_gain2, d_shift2 = norm_back(mm_nt(d_pre, w_up), n2, r2, gains[2])
    g = g + row

    gb = g.astype(BF)
    d_out_bias1 = colsum(gb)
    d_out1 = mm_tn(gb, o1)
    do = mm_nt(gb, w_out[1]).astype(BF)
    dq, dk, dv = attend_backward(q1, k1, v1, heard, kept1, do)
    d_q1 = mm_tn(h1, dq) * scale
    d_k1 = mm_tn(frames, dk)
    d_v1 = mm_tn(frames, dv)
    d_qb1 = colsum(dq) * scale
    d_vb1 = colsum(dv)
    row, d_gain1, d_shift1 = norm_back(mm_nt(dq, w_in[1, 0]) * scale, n1, r1, gains[1])
    g = g + row

    gb = g.astype(BF)
    d_out_bias0 = colsum(gb)
    d_out0 = mm_tn(gb, o0)
    do = mm_nt(gb, w_out[0]).astype(BF)
    dq, dk, dv = attend_backward(q0, k0, v0, causal, kept0, do)
    d_q0 = mm_tn(h0, dq) * scale
    d_k0 = mm_tn(h0, dk)
    d_v0 = mm_tn(h0, dv)
    d_qb0 = colsum(dq) * scale
    d_vb0 = colsum(dv)
    dh = mm_nt(dq, w_in[0, 0]) * scale + mm_nt(dk, w_in[0, 1]) + mm_nt(dv, w_in[0, 2])
    row, d_gain0, d_shift0 = norm_back(dh, n0, r0, gains[0])
    g = g + row
    input_grad = g.astype(BF)

    def reduced(grads):
        cols = [v.shape[1] // 2 for v in grads]
        sent = [v[:, c:].astype(BF) for v, c in zip(grads, cols)]
        got = [lax.ppermute(v, "tensor", other) for v in sent]
        pair = [(v[:, :c] + w.astype(F32)).astype(BF) for v, w, c in zip(grads, got, cols)]
        half = len(pair) // 2
        sums = []
        for flip, group_of in ((False, pair[:half]), (True, pair[half:])):
            sums.append(scatter_rows(jnp.concatenate(group_of, 1), flip).astype(F32))
        total = jnp.concatenate(sums, 1)
        at, pieces = 0, []
        for c in cols:
            pieces.append(total[:, at : at + c])
            at += c
        return pieces

    s_down, s_up = reduced([d_down, d_up])
    s_out1, s_q1, s_k1, s_v1 = reduced([d_out1, d_q1, d_k1, d_v1])
    s_out0, s_q0, s_k0, s_v0 = reduced([d_out0, d_q0, d_k0, d_v0])

    full = [
        jnp.stack([d_gain0, d_gain1, d_gain2]),
        jnp.stack([d_shift0, d_shift1, d_shift2]),
        jnp.stack([d_out_bias0, d_out_bias1]),
        d_down_bias,
        d_last_gain,
        d_last_shift,
        jnp.stack([square0, square1, text_count.astype(F32)]),
    ]
    halved = [jnp.stack([jnp.stack([d_qb0, d_vb0]), jnp.stack([d_qb1, d_vb1])]), d_up_bias]
    flat = jnp.concatenate([v.reshape(-1) for v in full])
    own = jnp.concatenate([v[..., : v.shape[-1] // 2].reshape(-1) for v in halved])
    far = jnp.concatenate([v[..., v.shape[-1] // 2 :].reshape(-1) for v in halved])
    got = lax.ppermute(jnp.concatenate([flat, far]), "tensor", other)
    total = sum_all(jnp.concatenate([flat, own]) + got)
    at, pieces = 0, []
    for v in full:
        pieces.append(total[at : at + v.size].reshape(v.shape))
        at += v.size
    for v in halved:
        shape = v.shape[:-1] + (v.shape[-1] // 2,)
        count = v.size // 2
        pieces.append(total[at : at + count].reshape(shape))
        at += count
    s_gain, s_shift, s_out_bias, s_down_bias, s_last_gain, s_last_shift, tail, s_qv, s_up_bias = pieces
    rms = jnp.sqrt(tail[:2] / (tail[2] * width))

    def pair_rows(mine):
        theirs = lax.ppermute(mine, "tensor", other)
        return jnp.where(core == 0, jnp.stack([mine, theirs]), jnp.stack([theirs, mine]))

    s_in = jnp.stack([jnp.stack([s_q0, s_k0, s_v0]), jnp.stack([s_q1, s_k1, s_v1])])
    s_out = jnp.stack([s_out0.T, s_out1.T])
    return (
        pair_rows(decoded),
        pair_rows(input_grad),
        rms,
        s_gain[None],
        s_shift[None],
        s_in[None],
        s_qv[None],
        s_out[None],
        s_out_bias[None],
        s_up[None],
        s_up_bias[None],
        s_down.T[None],
        s_down_bias[None],
        s_last_gain,
        s_last_shift,
    )


def solution(mesh):
    rows = ("dp", "section")
    return jax.shard_map(
        per_device,
        mesh=mesh,
        in_specs=(
            P(rows, None, None),
            P("dp", "section", None),
            P(rows, None, None),
            P(rows),
            P(rows),
            P(rows),
            P(),
            P(),
            P(),
            P(None, None, None, None, "tensor"),
            P(None, None, None, "tensor"),
            P(None, None, "tensor", None),
            P(),
            P(None, None, "tensor"),
            P(None, "tensor"),
            P(None, "tensor", None),
            P(),
            P(),
            P(),
        ),
        out_specs=(
            P(rows, None, None),
            P(rows, None, None),
            P(),
            P(),
            P(),
            P(None, None, None, rows, "tensor"),
            P(None, None, None, "tensor"),
            P(None, None, "tensor", rows),
            P(),
            P(None, rows, "tensor"),
            P(None, "tensor"),
            P(None, "tensor", rows),
            P(),
            P(),
            P(),
        ),
        check_vma=False,
    )
```

```python
import functools
import jax
import jax.numpy as jnp
from jax import lax
from jax.experimental import pallas as pl
from jax.experimental.pallas import tpu as pltpu
from jax.sharding import PartitionSpec as P

HEAD = 64
EPS = 1e-05
NEGATIVE = -1e30
BF = jnp.bfloat16
F32 = jnp.float32
VM = pltpu.VMEM
MEGA = 1 << 20
SCALE = HEAD ** (-0.5)
SMALL = 24


def dot(a, b):
    return jnp.dot(a, b, preferred_element_type=F32)


def dot_nt(a, b):
    return lax.dot_general(a, b, (((1,), (1,)), ((), ())), preferred_element_type=F32)


def dot_tn(a, b):
    return lax.dot_general(a, b, (((0,), (0,)), ((), ())), preferred_element_type=F32)


def norm_parts(rows):
    centred = rows - jnp.mean(rows, -1, keepdims=True)
    rstd = lax.rsqrt(jnp.mean(centred * centred, -1, keepdims=True) + EPS)
    return centred * rstd, rstd


def norm_back(grad, normal, rstd, gain):
    scaled = grad * gain
    row = rstd * (
        scaled
        - jnp.mean(scaled, -1, keepdims=True)
        - normal * jnp.mean(scaled * normal, -1, keepdims=True)
    )
    return row, jnp.sum(grad * normal, 0, keepdims=True), jnp.sum(grad, 0, keepdims=True)


def colsum(values):
    return jnp.sum(values.astype(F32), 0, keepdims=True)


def lanes(shape):
    return lax.broadcasted_iota(jnp.int32, shape, len(shape) - 1)


def split3(row):
    high = row.astype(BF)
    rest = row - high.astype(F32)
    mid = rest.astype(BF)
    return high, mid, (rest - mid.astype(F32)).astype(BF)


def extension(rows, bias):
    lane = lanes((rows, 128))
    return jnp.where(lane < 3, 1.0, jnp.where(lane == 3, bias, 0.0)).astype(BF)


def augmented(pair_t, head, row, last):
    cols = pair_t.shape[1]
    zero = jnp.zeros((HEAD, cols), BF)
    own = pair_t[head * HEAD : (head + 1) * HEAD]
    high, mid, low = split3(-row)
    sub = lax.broadcasted_iota(jnp.int32, (16, cols), 0)
    pick = lambda n, v: jnp.where(sub == n, jnp.broadcast_to(v.astype(F32), (16, cols)), 0.0)
    extra = pick(0, high) + pick(1, mid) + pick(2, low) + jnp.where(sub == 3, last, 0.0)
    parts = [own, zero] if head == 0 else [zero, own]
    return jnp.concatenate(
        parts + [extra.astype(BF), jnp.zeros((112, cols), BF)], axis=0
    )


def flip(values):
    return values.astype(F32).T


def whole(shape):
    return pl.BlockSpec(shape, lambda *_: (0,) * len(shape))


SMEM = pl.BlockSpec(memory_space=pltpu.SMEM)


def call(kernel, name, grid, in_specs, out_specs, out_shape, scratch=(), prefetch=0, flops=0):
    return pl.pallas_call(
        kernel,
        grid_spec=pltpu.PrefetchScalarGridSpec(
            num_scalar_prefetch=prefetch,
            grid=grid,
            in_specs=in_specs,
            out_specs=out_specs,
            scratch_shapes=list(scratch),
        ),
        out_shape=[jax.ShapeDtypeStruct(s, d) for s, d in out_shape],
        compiler_params=pltpu.CompilerParams(vmem_limit_bytes=56 * MEGA),
        cost_estimate=pl.CostEstimate(flops=flops, bytes_accessed=0, transcendentals=0)
        if flops
        else None,
        name=name,
    )


def self_forward_kernel(
    ids, text, hid, ng, nb, w_in, w_cq, w_out, qvb, ob,
    x1_ref, h0_ref, q_ref, k_ref, v_ref, o_ref, lse_ref, h1_ref, q1_ref, q1t_ref, sm_ref,
):
    count = text[ids[0]]
    x0 = hid[0].astype(F32)
    rows, width = x0.shape
    where_row = lax.broadcasted_iota(jnp.int32, (rows, 1), 0)
    valid = jnp.where(where_row < count, 1.0, 0.0)
    square = jnp.sum(jnp.sum(valid * (x0 * x0), -1, keepdims=True), 0, keepdims=True)
    lane = lanes((1, width))
    sm_ref[...] = jnp.zeros_like(sm_ref)
    sm_ref[11:12, :] = jnp.where(
        lane == 0, square, jnp.where(lane == 2, count.astype(F32), 0.0)
    )
    n, _ = norm_parts(x0)
    h = (n * ng[0:1, :].astype(F32) + nb[0:1, :].astype(F32)).astype(BF)
    h0_ref[...] = h
    q_ref[...] = ((dot(h, w_in[0, 0]) + qvb[0:1, :].astype(F32)) * SCALE).astype(BF)
    k_ref[...] = dot(h, w_in[0, 1]).astype(BF)
    v_ref[...] = (dot(h, w_in[0, 2]) + qvb[1:2, :].astype(F32)).astype(BF)
    cut = 256
    rest = rows - cut
    behind = lax.broadcasted_iota(jnp.int32, (cut, cut), 0) > lax.broadcasted_iota(
        jnp.int32, (cut, cut), 1
    )
    tri = jnp.where(behind, NEGATIVE, 0.0)
    lse_ref[...] = jnp.zeros_like(lse_ref)
    for pair in range(width // 128):
        cols = pl.ds(pair * 128, 128)
        q_t = flip(q_ref[:, cols]).astype(BF)
        v_t = flip(v_ref[:, cols]).astype(BF)
        k = k_ref[:, cols]
        zero = jnp.zeros((HEAD, rows), BF)
        outs = []
        for head in range(2):
            span = slice(head * HEAD, (head + 1) * HEAD)
            own = q_t[span]
            own = jnp.concatenate([own, zero] if head == 0 else [zero, own], axis=0)
            high = dot(k[0:cut], own)
            early = high[:, 0:cut] + tri
            late = high[:, cut:]
            low = dot(k[cut:], own[:, cut:]) + tri[0:rest, 0:rest]
            peak0 = jnp.max(early, 0, keepdims=True)
            peak1 = jnp.maximum(
                jnp.max(late, 0, keepdims=True), jnp.max(low, 0, keepdims=True)
            )
            early = jnp.exp(early - peak0)
            late = jnp.exp(late - peak1)
            low = jnp.exp(low - peak1)
            total0 = jnp.sum(early, 0, keepdims=True)
            total1 = jnp.sum(late, 0, keepdims=True) + jnp.sum(low, 0, keepdims=True)
            mix0 = dot(v_t[span, 0:cut], early.astype(BF)) * (1.0 / total0)
            mix1 = dot(v_t[span, 0:cut], late.astype(BF)) + dot(v_t[span, cut:], low.astype(BF))
            mix1 = mix1 * (1.0 / total1)
            outs.append(jnp.concatenate([mix0, mix1], axis=1))
            at = 2 * pair + head
            lse_ref[at : at + 1, 0:cut] = peak0 + jnp.log(total0)
            lse_ref[at : at + 1, cut:] = peak1 + jnp.log(total1)
        o_ref[:, cols] = jnp.concatenate(outs, axis=0).T.astype(BF)
    x1 = x0 + (dot(o_ref[...], w_out[0]) + ob[0:1, :].astype(F32))
    x1_ref[...] = x1
    n, _ = norm_parts(x1)
    h = (n * ng[1:2, :].astype(F32) + nb[1:2, :].astype(F32)).astype(BF)
    h1_ref[...] = h
    q1 = ((dot(h, w_cq[0, 0]) + qvb[2:3, :].astype(F32)) * SCALE).astype(BF)
    q1_ref[...] = q1
    q1t_ref[...] = flip(q1).astype(BF)


def self_forward(ids, text, hidden, ng, nb, w_in, w_out, qvb, ob):
    _, rows, width = hidden.shape
    block = (rows, width)
    b16 = [(block, BF)]
    return call(
        self_forward_kernel, "self_forward", (1,),
        [SMEM, pl.BlockSpec((1, rows, width), lambda i, s: (s[0], 0, 0)), whole(ng.shape), whole(nb.shape),
         pl.BlockSpec((1, 3, width, width), lambda i, s: (0, 0, 0, 0)),
         pl.BlockSpec((1, 1, width, width), lambda i, s: (1, 0, 0, 0)),
         pl.BlockSpec((1, width, width), lambda i, s: (0, 0, 0)), whole(qvb.shape), whole(ob.shape)],
        [whole(block)] * 6 + [whole((16, rows))] + [whole(block)] * 2
        + [whole((width, rows)), whole((SMALL, width))],
        [(block, F32)] + b16 * 5 + [((16, rows), F32)] + b16 * 2
        + [((width, rows), BF), ((SMALL, width), F32)],
        prefetch=1, flops=5 * 2 * rows * width * width,
    )(ids, text, hidden, ng, nb, w_in, w_in, w_out, qvb, ob)


def cross_block_kernel(first, last, ids, audio, *refs):
    refs = list(refs)
    q_ref, f_ref, w_in, qvb = refs[:4]
    del refs[:4]
    if not first:
        acc_in, st_in = refs[:2]
        del refs[:2]
    if last:
        x1_ref, w_out, ob = refs[:3]
        del refs[:3]
    k_ref, v_ref = refs[:2]
    if last:
        x2_ref, o_ref, lse_ref = refs[2:]
        lse_ref[...] = jnp.zeros_like(lse_ref)
    else:
        acc, st = refs[2:]
        st[...] = jnp.zeros_like(st)
    size, width = f_ref.shape
    rows = q_ref.shape[1]
    frames = f_ref[...]
    k_ref[...] = dot(frames, w_in[0, 1]).astype(BF)
    v_ref[...] = (dot(frames, w_in[0, 2]) + qvb[3:4, :].astype(F32)).astype(BF)
    slot = ids[1] * size + lax.broadcasted_iota(jnp.int32, (size, 1), 0)
    ext = extension(size, jnp.where(slot < audio[ids[0]], 0.0, NEGATIVE))
    sub = lax.broadcasted_iota(jnp.int32, (128, rows), 0)
    one = jnp.where(sub == 3, 1.0, 0.0).astype(BF)
    zero = jnp.zeros((HEAD, rows), BF)
    for pair in range(width // 128):
        cols = pl.ds(pair * 128, 128)
        k = jnp.concatenate([k_ref[:, cols], ext], axis=1)
        v_t = flip(v_ref[:, cols]).astype(BF)
        outs = []
        for head in range(2):
            at = 2 * pair + head
            own = q_ref[at * HEAD : (at + 1) * HEAD, :]
            s = dot(k, jnp.concatenate([own, zero, one] if head == 0 else [zero, own, one], axis=0))
            peak = jnp.max(s, 0, keepdims=True)
            if not first:
                old = st_in[at : at + 1, :]
                peak = jnp.maximum(peak, old)
                fade = jnp.exp(old - peak)
            e = jnp.exp(s - peak)
            total = jnp.sum(e, 0, keepdims=True)
            mix = dot(v_t[head * HEAD : (head + 1) * HEAD], e.astype(BF))
            if not first:
                total += fade * st_in[16 + at : 17 + at, :]
                mix += fade * acc_in[at * HEAD : (at + 1) * HEAD, :]
            if last:
                outs.append(mix * (1.0 / total))
                lse_ref[at : at + 1, :] = peak + jnp.log(total)
            else:
                acc[at * HEAD : (at + 1) * HEAD, :] = mix
                st[at : at + 1, :] = peak
                st[16 + at : 17 + at, :] = total
        if last:
            o_ref[:, cols] = jnp.concatenate(outs, axis=0).T.astype(BF)
    if last:
        x2_ref[...] = x1_ref[...] + (dot(o_ref[...], w_out[0]) + ob[1:2, :].astype(F32))


def cross_block(ids, audio, q1, frames, w_in, qvb, state=None, tail=None):
    size, width = frames.shape
    rows = q1.shape[1]
    block = (rows, width)
    specs = [SMEM, whole(q1.shape), whole(frames.shape),
             pl.BlockSpec((1, 3, width, width), lambda i, s: (1, 0, 0, 0)), whole(qvb.shape)]
    args = [audio, q1, frames, w_in, qvb]
    if state is not None:
        specs += [whole(q1.shape), whole((32, rows))]
        args += list(state)
    outs = [((size, width), BF)] * 2
    if tail is not None:
        x1, w_out, ob = tail
        specs += [whole(block), pl.BlockSpec((1, width, width), lambda i, s: (1, 0, 0)), whole(ob.shape)]
        args += [x1, w_out, ob]
        outs += [(block, F32), (block, BF), ((16, rows), F32)]
    else:
        outs += [(q1.shape, F32), ((32, rows), F32)]
    return call(
        functools.partial(cross_block_kernel, state is None, tail is not None),
        "cross_block", (1,), specs, [whole(s) for s, _ in outs], outs,
        prefetch=1, flops=12 * size * width * width,
    )(ids, *args)


def gelu_parts(a):
    z = jnp.abs(a) * 0.7071067811865476
    t = 1.0 / (1.0 + 0.3275911 * z)
    e = jnp.exp(a * a * -0.5)
    poly = t * (
        0.254829592
        + t * (-0.284496736 + t * (1.421413741 + t * (-1.453152027 + t * 1.061405429)))
    )
    q = 0.5 * poly * e
    phi = jnp.where(a < 0, q, 1.0 - q)
    return a * phi, phi + a * e * 0.3989422804014327


def feed_forward_kernel(
    steps, ids, text, group, gw, x2_ref, og_ref, ng_ref, nb_ref, fg_ref, fb_ref,
    w1l, w1r, b1l, b1r, w2l, w2r, b2_ref, sm_in,
    dec_ref, gb_ref, g_ref, h2_ref, slope_l, slope_r, d2l, d2r, sm_ref,
    us_l, us_r, acc, keep,
):
    i = pl.program_id(0)

    @pl.when(i == 0)
    def _():
        n, r = norm_parts(x2_ref[...])
        h2_ref[...] = (n * ng_ref[2:3, :].astype(F32) + nb_ref[2:3, :].astype(F32)).astype(BF)
        acc[...] = x2_ref[...] + b2_ref[...].astype(F32)
        sm_ref[...] = sm_in[...]

    @pl.when(i < steps)
    def _():
        total = acc[...]
        for w1, b1, w2, us, slope in (
            (w1l, b1l, w2l, us_l, slope_l),
            (w1r, b1r, w2r, us_r, slope_r),
        ):
            u, s = gelu_parts(dot(h2_ref[...], w1[...]) + b1[...].astype(F32))
            u = u.astype(BF)
            us[i] = u
            slope[...] = s.astype(BF)
            total += dot(u, w2[...])
        acc[...] = total

    @pl.when(i == steps - 1)
    def _():
        x3 = acc[...]
        rows = lax.broadcasted_iota(jnp.int32, (x3.shape[0], 1), 0)
        core = ids[0]
        valid = jnp.where(rows < text[core], 1.0, 0.0)
        n, r = norm_parts(x3)
        gain = fg_ref[...].astype(F32)
        dec_ref[...] = (n * gain + fb_ref[...].astype(F32)).astype(BF)
        c = og_ref[0].astype(F32) * (valid * gw[group[core]])
        g, dg, db = norm_back(c, n, r, gain)
        gb = g.astype(BF)
        g_ref[...] = g
        gb_ref[...] = gb
        keep[...] = flip(gb).astype(BF)
        sm_ref[9:10, :] = dg
        sm_ref[10:11, :] = db
        sm_ref[8:9, :] = colsum(gb)
        square = jnp.sum(jnp.sum(valid * (x3 * x3), -1, keepdims=True), 0, keepdims=True)
        sm_ref[11:12, :] = jnp.where(lanes((1, x3.shape[1])) == 1, square, sm_ref[11:12, :])

    @pl.when(i >= steps)
    def _():
        d2l[...] = dot(keep[...], us_l[i - steps]).astype(BF)
        d2r[...] = dot(keep[...], us_r[i - steps]).astype(BF)


def feed_forward(ids, text, group, gw, x2, og, ng, nb, fg, fb, w1l, w1r, b1l, b1r, w2l, w2r, b2, sm, block=512):
    rows, width = x2.shape
    half = w1l.shape[1]
    steps = half // block
    ph1 = lambda i: jnp.minimum(i, steps - 1)
    ph2 = lambda i: jnp.maximum(i - steps, 0)
    colspec = pl.BlockSpec((width, block), lambda i, s: (0, ph1(i)))
    bspec = pl.BlockSpec((1, block), lambda i, s: (0, ph1(i)))
    rowspec = pl.BlockSpec((block, width), lambda i, s: (ph1(i), 0))
    outd = pl.BlockSpec((width, block), lambda i, s: (0, ph2(i)))
    slope = pl.BlockSpec((rows, block), lambda i, s: (0, ph1(i)))
    full = whole((rows, width))
    return call(
        functools.partial(feed_forward_kernel, steps), "feed_forward", (2 * steps,),
        [SMEM, SMEM, SMEM, full, pl.BlockSpec((1, rows, width), lambda i, s: (s[0], 0, 0)),
         whole(ng.shape), whole(nb.shape), whole(fg.shape), whole(fb.shape),
         colspec, colspec, bspec, bspec, rowspec, rowspec, whole(b2.shape), whole(sm.shape)],
        [full, full, full, full, slope, slope, outd, outd, whole(sm.shape)],
        [((rows, width), BF), ((rows, width), BF), ((rows, width), F32), ((rows, width), BF),
         ((rows, half), BF), ((rows, half), BF), ((width, half), BF), ((width, half), BF), (sm.shape, F32)],
        scratch=[VM((steps, rows, block), BF), VM((steps, rows, block), BF), VM((rows, width), F32), VM((width, rows), BF)],
        prefetch=1, flops=3 * 4 * rows * width * half,
    )(ids, text, group, gw, x2, og, ng, nb, fg, fb, w1l, w1r, b1l, b1r, w2l, w2r, b2, sm)


def feed_back_kernel(
    steps, gb_ref, g_ref, h2_ref, x2_ref, ng_ref, w1l, w1r, w2l, w2r, slope_l, slope_r, sm_in,
    gout, d1l, d1r, db1l, db1r, sm_ref, keep, dh,
):
    i = pl.program_id(0)

    @pl.when(i == 0)
    def _():
        keep[...] = flip(h2_ref[...]).astype(BF)
        dh[...] = jnp.zeros_like(dh)
        sm_ref[...] = sm_in[...]

    total = dh[...]
    for w1, w2, slope, d1, db1 in ((w1r, w2r, slope_r, d1r, db1r), (w1l, w2l, slope_l, d1l, db1l)):
        da = (dot_nt(gb_ref[...], w2[...]) * slope[...].astype(F32)).astype(BF)
        db1[...] = colsum(da)
        d1[...] = dot(keep[...], da).astype(BF)
        total += dot_nt(da, w1[...])
    dh[...] = total

    @pl.when(i == steps - 1)
    def _():
        n, r = norm_parts(x2_ref[...])
        row, dg, db = norm_back(dh[...], n, r, ng_ref[2:3, :].astype(F32))
        gout[...] = g_ref[...] + row
        sm_ref[2:3, :] = dg
        sm_ref[5:6, :] = db


def feed_back(gb, g, h2, x2, ng, w1l, w1r, w2l, w2r, slope_l, slope_r, sm, block=512):
    rows, width = x2.shape
    half = w1l.shape[1]
    steps = half // block
    full = whole((rows, width))
    colspec = pl.BlockSpec((width, block), lambda i: (0, i))
    bspec = pl.BlockSpec((1, block), lambda i: (0, i))
    rowspec = pl.BlockSpec((block, width), lambda i: (i, 0))
    slope = pl.BlockSpec((rows, block), lambda i: (0, i))
    return call(
        functools.partial(feed_back_kernel, steps), "feed_back", (steps,),
        [full, full, full, full, whole(ng.shape), colspec, colspec, rowspec, rowspec, slope, slope, whole(sm.shape)],
        [full, colspec, colspec, bspec, bspec, whole(sm.shape)],
        [((rows, width), F32), ((width, half), BF), ((width, half), BF), ((1, half), F32), ((1, half), F32), (sm.shape, F32)],
        scratch=[VM((width, rows), BF), VM((rows, width), F32)], flops=3 * 4 * rows * width * half,
    )(gb, g, h2, x2, ng, w1l, w1r, w2l, w2r, slope_l, slope_r, sm)


def attention_back_kernel(index, causal, blocks, pairs, ids, audio, *refs):
    refs = list(refs)
    take = lambda n: [refs.pop(0) for _ in range(n)]
    g_ref, x_ref, ng_ref, w_out, q_ref, o_ref, lse_ref, w_q, sm_in = take(9)
    ks, vs = take(blocks), take(blocks)
    if causal:
        w_k, w_v = take(2)
    gout, gb_ref, dq_ref = take(3)
    dks, dvs = take(blocks), take(blocks)
    (sm_ref,) = take(1)
    dqs = take(1)[0]
    exts = take(blocks)
    if causal:
        tri, dkall, dvall = take(3)
    rows, width = g_ref.shape
    step = pl.program_id(0)

    @pl.when(step == 0)
    def _():
        gb = g_ref[...].astype(BF)
        gb_ref[...] = gb
        sm_ref[...] = sm_in[...]
        sm_ref[6 + index : 7 + index, :] = colsum(gb)
        if causal:
            exts[0][...] = extension(rows, 0.0)
            cut = 256
            far = lax.broadcasted_iota(jnp.int32, (cut, rows), 0) > lax.broadcasted_iota(
                jnp.int32, (cut, rows), 1
            )
            tri[...] = jnp.where(far, NEGATIVE, 0.0)
        else:
            for n in range(blocks):
                size = ks[n].shape[0]
                slot = ids[1 + n] * size + lax.broadcasted_iota(jnp.int32, (size, 1), 0)
                exts[n][...] = extension(size, jnp.where(slot < audio[ids[0]], 0.0, NEGATIVE))

    lane = lanes((rows, 128))
    do_t = dot_nt(w_out[0], gb_ref[...]).astype(BF)
    do = flip(do_t).astype(BF)
    both = do_t.astype(F32) * flip(o_ref[...])
    q = q_ref[...]
    q_t = flip(q).astype(BF)
    q_aug, do_aug, q_own, do_own = [], [], [], []
    for head in range(2):
        mine = (lane < HEAD) if head == 0 else (lane >= HEAD)
        lse = lse_ref[pl.ds(2 * step + head, 1), :]
        delta = jnp.sum(both[head * HEAD : (head + 1) * HEAD], 0, keepdims=True)
        q_aug.append(augmented(q_t, head, lse, 1.0))
        do_aug.append(augmented(do_t, head, delta, 0.0))
        q_own.append(jnp.where(mine, q, jnp.zeros_like(q)))
        do_own.append(jnp.where(mine, do, jnp.zeros_like(do)))
    if causal:
        cut = 256
        tiles = [(0, 0, cut, 0), (0, cut, rows - cut, cut)]
    else:
        tiles = [(n, 0, ks[n].shape[0], 0) for n in range(blocks)]
    dq_t = [None, None]
    for n, top, size, left in tiles:
        span = pl.ds(top, size)
        k = ks[n][span, :]
        ext = exts[n][span, :]
        k_aug = jnp.concatenate([k, ext], axis=1)
        v_aug = jnp.concatenate([vs[n][span, :], ext], axis=1)
        k_t = flip(k).astype(BF)
        dk = dv = None
        for head in range(2):
            s = dot(k_aug, q_aug[head][:, left:])
            if causal:
                s = s + tri[0:size, 0 : rows - left]
            p = jnp.exp(s)
            ds = (p * dot(v_aug, do_aug[head][:, left:])).astype(BF)
            part = dot(p.astype(BF), do_own[head][left:])
            dv = part if dv is None else dv + part
            part = dot(ds, q_own[head][left:])
            dk = part if dk is None else dk + part
            part = dot(k_t[head * HEAD : (head + 1) * HEAD], ds)
            if left:
                part = jnp.concatenate([jnp.zeros((HEAD, left), F32), part], axis=1)
            dq_t[head] = part if dq_t[head] is None else dq_t[head] + part
        dk = dk.astype(BF)
        dv = dv.astype(BF)
        dks[n][span, :] = dk
        dvs[n][span, :] = dv
        if causal:
            dkall[step, span, :] = dk
            dvall[step, span, :] = dv
        total = colsum(dv)
        sums = total if n == 0 and top == 0 else sums + total
    dq = jnp.concatenate(dq_t, axis=0).T.astype(BF)
    dq_ref[...] = dq
    dqs[step] = dq
    qsum = colsum(dq) * SCALE
    own = pairs // 2
    for pair in range(pairs):

        @pl.when(step == pair)
        def _():
            row = (12 if pair < own else 16) + index
            at = (pair % own) * 128
            sm_ref[row : row + 1, at : at + 128] = qsum
            sm_ref[row : row + 1, own * 128 + at : own * 128 + at + 128] = sums

    @pl.when(step == pairs - 1)
    def _():
        dq = jnp.concatenate([dqs[n] for n in range(pairs)], axis=1)
        dh = dot_nt(dq, w_q[0, 0]) * SCALE
        if causal:
            dh += dot_nt(jnp.concatenate([dkall[n] for n in range(pairs)], axis=1), w_k[0, 0])
            dh += dot_nt(jnp.concatenate([dvall[n] for n in range(pairs)], axis=1), w_v[0, 0])
        x = x_ref[0].astype(F32) if causal else x_ref[...]
        n, r = norm_parts(x)
        row, dg, db = norm_back(dh, n, r, ng_ref[index : index + 1, :].astype(F32))
        gout[...] = (g_ref[...] + row).astype(gout.dtype)
        sm_ref[index : index + 1, :] = dg
        sm_ref[3 + index : 4 + index, :] = db


def attention_back(ids, audio, g, x, ng, w_in, w_out, q, o, lse, sm, ks, vs, causal):
    rows, width = g.shape
    pairs = width // 128
    index = 0 if causal else 1
    blocks = len(ks)
    full = whole((rows, width))
    col = pl.BlockSpec((rows, 128), lambda i, s: (0, i))
    weight = lambda m: pl.BlockSpec((1, 1, width, width), lambda i, s, m=m: (index, m, 0, 0))
    kv = [pl.BlockSpec((k.shape[0], 128), lambda i, s: (0, i)) for k in ks]
    x_spec = pl.BlockSpec((1, rows, width), lambda i, s: (s[0], 0, 0)) if causal else full
    specs = [SMEM, full, x_spec, whole(ng.shape), pl.BlockSpec((1, 128, width), lambda i, s: (index, i, 0)),
             col, col, whole(lse.shape), weight(0), whole(sm.shape)] + kv + kv
    args = [audio, g, x, ng, w_out, q, o, lse, w_in, sm, *ks, *vs]
    scratch = [VM((pairs, rows, 128), BF)] + [VM((k.shape[0], 128), BF) for k in ks]
    if causal:
        specs += [weight(1), weight(2)]
        args += [w_in, w_in]
        scratch += [VM((256, rows), F32), VM((pairs, rows, 128), BF), VM((pairs, rows, 128), BF)]
    shapes = [(rows, width)] * 3 + [k.shape for k in ks] * 2 + [sm.shape]
    types = [BF if causal else F32, BF, BF] + [BF] * (2 * blocks) + [F32]
    return call(
        functools.partial(attention_back_kernel, index, causal, blocks, pairs),
        "self_back" if causal else "cross_back", (pairs,), specs,
        [full, full, col] + kv + kv + [whole(sm.shape)], list(zip(shapes, types)),
        scratch=scratch, prefetch=1, flops=10 * rows * width * sum(k.shape[0] for k in ks) * 2,
    )(ids, *args)


def weight_grad_kernel(blocks, self_src, *refs):
    refs = list(refs)
    take = lambda n: [refs.pop(0) for _ in range(n)]
    gb, h, o, dq = take(4)
    src = [h] if self_src else take(blocks)
    dks, dvs = take(blocks), take(blocks)
    a_ref, b_ref = refs
    half = o.shape[1]
    a_ref[:, 0:half] = dot_tn(gb[...], o[...]).astype(BF)
    a_ref[:, half:] = (dot_tn(h[...], dq[...]) * SCALE).astype(BF)
    total = None
    for f, dk, dv in zip(src, dks, dvs):
        part = dot_tn(f[...], jnp.concatenate([dk[...], dv[...]], axis=1))
        total = part if total is None else total + part
    b_ref[...] = total.astype(BF)


def weight_grad(side, gb, h, o, dq, frames, dks, dvs, block=256):
    rows, width = h.shape
    half = width // 2
    blocks = len(dks)
    left = lambda n: pl.BlockSpec((n, block), lambda i: (0, i))
    right = lambda n: pl.BlockSpec((n, half), lambda i: (0, side))
    srcs = [] if frames is None else list(frames)
    specs = [left(rows), left(rows), right(rows), right(rows)] + [left(f.shape[0]) for f in srcs]
    specs += [right(k.shape[0]) for k in dks] * 2
    out = pl.BlockSpec((block, 2 * half), lambda i: (i, 0))
    return call(
        functools.partial(weight_grad_kernel, blocks, frames is None),
        "cross_weights" if srcs else "self_weights", (width // block,), specs, [out, out],
        [((width, 2 * half), BF)] * 2,
        flops=2 * width * half * 2 * (rows + sum(k.shape[0] for k in dks)),
    )(gb, h, o, dq, *srcs, *dks, *dvs)


def swap(axis, bit):
    return [(i, i ^ (1 << bit)) for i in range(lax.axis_size(axis))]


def bits_of(axis):
    return (lax.axis_size(axis) - 1).bit_length()


def pick(values, axis, index):
    return lax.dynamic_index_in_dim(values, index, axis, keepdims=False)


def scatter_rows(parts, flipped):
    dims = [("dp", b) for b in reversed(range(bits_of("dp")))]
    dims += [("section", b) for b in reversed(range(bits_of("section")))]
    rows, cols = parts[0].shape
    share = rows >> len(dims)
    cubes = [v.reshape((2,) * len(dims) + (share, cols)) for v in parts]
    order = [d for d in dims if d[0] == "dp"]
    if not flipped:
        order = order[::-1]
    for axis, bit in order + [d for d in dims if d[0] == "section"][::-1]:
        where = dims.index((axis, bit))
        mine = (lax.axis_index(axis) >> bit) & 1
        sent = sum(pick(c, where, 1 - mine).astype(F32) for c in cubes).astype(BF)
        got = lax.ppermute(sent, axis, swap(axis, bit))
        cubes = [pick(c, where, mine) for c in cubes] + [got]
        dims.remove((axis, bit))
    return sum(c.astype(F32) for c in cubes)


def per_device(
    hidden,
    enc_states,
    out_grad,
    text_len,
    audio_len,
    group_id,
    group_weight,
    norm_gain,
    norm_bias,
    attention_in,
    query_value_bias,
    attention_out,
    attention_out_bias,
    mlp_in,
    mlp_in_bias,
    mlp_out,
    mlp_out_bias,
    final_gain,
    final_bias,
):
    width = hidden.shape[2]
    sections = lax.axis_size("section")
    core = lax.axis_index("tensor")
    section = lax.axis_index("section")
    other = swap("tensor", 0)
    half = width // 2

    def far(values):
        return lax.ppermute(values, "tensor", other)

    steps = [0] + sorted(range(1, sections), key=lambda n: abs(2 * n - sections))
    frames = []
    for step in steps:
        target = lax.rem(section + step, sections)
        block = pick(enc_states, 0, 2 * target + core)
        if step:
            block = lax.ppermute(
                block, "section", [(i, (i + step) % sections) for i in range(sections)]
            )
        frames.append(block)
    sources = [lax.rem(section - step + sections, sections) for step in steps]
    ids = jnp.stack([core] + sources).astype(jnp.int32)
    block_ids = [jnp.stack([core, s]).astype(jnp.int32) for s in sources]

    w_in = jnp.concatenate([attention_in[0], far(attention_in)[0]], 3)
    w_out = jnp.concatenate([attention_out[0], far(attention_out)[0]], 1)
    qvb = jnp.concatenate([query_value_bias[0], far(query_value_bias)[0]], 2).reshape(4, width)
    w1l, w1r = mlp_in[0], far(mlp_in)[0]
    b1l, b1r = mlp_in_bias, far(mlp_in_bias)
    w2l, w2r = mlp_out[0], far(mlp_out)[0]
    ng, nb = norm_gain[0], norm_bias[0]
    ob = attention_out_bias[0]
    fg, fb = final_gain[None], final_bias[None]

    x1, h0, q0, k0, v0, o0, lse0, h1, q1, q1t, sm = self_forward(
        ids, text_len, hidden, ng, nb, w_in, w_out, qvb, ob
    )
    k1, v1, state = [], [], None
    for n, block in enumerate(frames):
        tail = (x1, w_out, ob) if n == sections - 1 else None
        r = cross_block(block_ids[n], audio_len, q1t, block, w_in, qvb, state, tail)
        k1.append(r[0])
        v1.append(r[1])
        state = r[2:4]
    x2, o1, lse1 = r[2:]
    decoded, gb, g, h2, slope_l, slope_r, d2l, d2r, sm = feed_forward(
        ids, text_len, group_id, group_weight, x2, out_grad, ng, nb, fg, fb,
        w1l, w1r, b1l, b1r, w2l, w2r, mlp_out_bias, sm,
    )
    down = scatter_rows([d2l, far(d2r)], False)
    g, d1l, d1r, db1l, db1r, sm = feed_back(
        gb, g, h2, x2, ng, w1l, w1r, w2l, w2r, slope_l, slope_r, sm
    )
    up = scatter_rows([d1l, far(d1r)], True)
    r = attention_back(ids, audio_len, g, x1, ng, w_in, w_out, q1, o1, lse1, sm, k1, v1, False)
    g, gb, dq = r[:3]
    dk, dv, sm = r[3 : 3 + sections], r[3 + sections : 3 + 2 * sections], r[-1]
    a_r, b_r = weight_grad(1, gb, h1, o1, dq, frames, dk, dv)
    a_l, b_l = weight_grad(0, gb, h1, o1, dq, frames, dk, dv)
    cross = [scatter_rows([a_l, far(a_r)], False), scatter_rows([b_l, far(b_r)], True)]
    input_grad, gb, dq, dk, dv, sm = attention_back(
        ids, audio_len, g, hidden, ng, w_in, w_out, q0, o0, lse0, sm, [k0], [v0], True
    )
    a_r, b_r = weight_grad(1, gb, h0, o0, dq, None, [dk], [dv])
    a_l, b_l = weight_grad(0, gb, h0, o0, dq, None, [dk], [dv])
    own = [scatter_rows([a_l, far(a_r)], False), scatter_rows([b_l, far(b_r)], True)]

    up_rows = mlp_in_bias.shape[1] // width
    sent = jnp.concatenate([sm[0:12], sm[16:18], db1r.reshape(up_rows, width)])
    kept = jnp.concatenate([sm[0:14], db1l.reshape(up_rows, width)])
    total = kept + far(sent)
    for axis in ("dp", "section"):
        for bit in range(bits_of(axis)):
            total = total + lax.ppermute(total, axis, swap(axis, bit))
    rms = jnp.sqrt(total[11, 0:2] / (total[11, 2] * width))

    def pair_rows(mine):
        theirs = far(mine)
        return jnp.where(core == 0, jnp.stack([mine, theirs]), jnp.stack([theirs, mine]))

    def matrices(pair):
        a, b = pair
        return jnp.stack([a[:, half:], b[:, :half], b[:, half:]]), a[:, :half].T

    in0, out0 = matrices(own)
    in1, out1 = matrices(cross)
    return (
        pair_rows(decoded),
        pair_rows(input_grad),
        rms,
        total[None, 0:3],
        total[None, 3:6],
        jnp.stack([in0, in1])[None],
        total[12:14].reshape(1, 2, 2, half),
        jnp.stack([out0, out1])[None],
        total[None, 6:8],
        up[None],
        total[12 + 2 :].reshape(1, -1),
        down.T[None],
        total[8:9],
        total[9],
        total[10],
    )


def solution(mesh):
    rows = ("dp", "section")
    return jax.shard_map(
        per_device,
        mesh=mesh,
        in_specs=(
            P(rows, None, None),
            P("dp", "section", None),
            P(rows, None, None),
            P(rows),
            P(rows),
            P(rows),
            P(),
            P(),
            P(),
            P(None, None, None, None, "tensor"),
            P(None, None, None, "tensor"),
            P(None, None, "tensor", None),
            P(),
            P(None, None, "tensor"),
            P(None, "tensor"),
            P(None, "tensor", None),
            P(),
            P(),
            P(),
        ),
        out_specs=(
            P(rows, None, None),
            P(rows, None, None),
            P(),
            P(),
            P(),
            P(None, None, None, rows, "tensor"),
            P(None, None, None, "tensor"),
            P(None, None, "tensor", rows),
            P(),
            P(None, rows, "tensor"),
            P(None, "tensor"),
            P(None, "tensor", rows),
            P(),
            P(),
            P(),
        ),
        check_vma=False,
    )
```
